128 devices in a mesh: shard: 16 (over z, x), rep: 8 (over y, core).
Axes of the slice: x: 4, y: 4, z: 4, core: 2. Of those that a mesh axis runs over, the one named last changes fastest.
Arguments:
- gradients: bfloat16 [8, 2048, 59392], P('rep', None, 'shard'), may hold values from -250 to 250
- keep_rows: int32 [8, 16, 464, 32], P('rep', None, 'shard'), may hold values from 0 to 127, as said below
- keep_counts: int32 [8, 16, 464], P('rep', None, 'shard'), may hold values from 16 to 32, as said below
- momentum: float32 [16, 128, 59392], P('rep', 'shard'), may hold values from -3 to 3
Outputs:
- new_momentum: float32 [16, 128, 59392], P('rep', 'shard')
The draws below stay inside these ranges and needn't reach their ends.
Inputs may be any that keep to these rules, and one draw needn't show every extreme that they name: In each tile of each replica the first keep_counts entries of keep_rows are distinct; later entries are not used. `keep_counts`: each replica has a tile with exactly 32 kept rows.
All inputs are finite; a program needn't handle non-finite values.
Results may differ from the reference program's by a relative error of at most 0.012.
Values may be sent and summed in bfloat16 or wider, within the bound.
A program may use at most 192 MiB of HBM per device.

```python
import math
import jax
import jax.numpy as jnp
from jax import lax

FF = 59392
TILE = 128
KMAX = 32
ROW_TILES = 16
ROWS = 2048
COL_TILES = 464
N_SHARD = 16
N_REP = 8


def draw_gradients(key, part):
    key = jax.random.fold_in(key, 11)
    key_noise = jax.random.fold_in(key, 0)
    key_rows = jax.random.fold_in(key, 1)
    key_cols = jax.random.fold_in(key, 2)
    key_band = jax.random.fold_in(key, 4)
    key_block = jax.random.fold_in(key, 5)
    band_width = FF // N_SHARD
    row_place = jnp.arange(ROWS, dtype=jnp.float32) / ROWS
    col_place = jnp.arange(FF, dtype=jnp.float32) / FF
    row_scale = jnp.exp(jax.random.uniform(key_rows, (ROWS,), minval=math.log(0.3), maxval=math.log(3.0))) * (1.0 + 0.75 * row_place)
    col_scale = jnp.exp(jax.random.uniform(key_cols, (FF,), minval=math.log(0.3), maxval=math.log(3.0))) * (1.0 + 0.75 * col_place)
    band_level = jnp.exp(jax.random.uniform(key_band, (N_SHARD,), minval=math.log(0.35), maxval=math.log(1.8)))
    block_level = jnp.exp(jax.random.uniform(key_block, (N_REP, ROW_TILES, N_SHARD), minval=math.log(0.35), maxval=math.log(1.8)))
    noise = jnp.clip(jax.random.normal(key_noise, (N_REP, ROWS, FF)), -5.0, 5.0)
    scaled = noise * row_scale[None, :, None] * col_scale[None, None, :]
    scaled = scaled.reshape(N_REP, ROW_TILES, TILE, N_SHARD, band_width)
    levels = block_level * band_level[None, None, :]
    scaled = scaled * levels[:, :, None, :, None]
    scaled = jnp.clip(scaled.reshape(N_REP, ROWS, FF), -250.0, 250.0)
    return scaled.astype(jnp.bfloat16)


def draw_keep_rows(key, part):
    key = jax.random.fold_in(key, 23)
    base = jnp.broadcast_to(jnp.arange(TILE, dtype=jnp.int32), (N_REP, ROW_TILES, COL_TILES, TILE))
    shuffled = jax.random.permutation(key, base, axis=3, independent=True)
    return shuffled[..., :KMAX]


def draw_keep_counts(key, part):
    key = jax.random.fold_in(key, 37)
    key_counts, key_place = jax.random.split(key, 2)
    counts = jax.random.randint(key_counts, (N_REP, ROW_TILES * COL_TILES), KMAX // 2, KMAX + 1)
    place = jax.random.randint(key_place, (N_REP,), 0, ROW_TILES * COL_TILES)
    chosen = jnp.arange(ROW_TILES * COL_TILES, dtype=jnp.int32)[None, :] == place[:, None]
    counts = jnp.where(chosen, KMAX, counts)
    return counts.reshape(N_REP, ROW_TILES, COL_TILES).astype(jnp.int32)


def block_levels(key, extent, cuts, smallest, largest):
    loudness = 1.0
    for dim, shards_of in cuts:
        steps = jax.random.uniform(jax.random.fold_in(jax.random.fold_in(key, 6), dim), (shards_of,), jnp.float32, smallest / len(cuts), largest / len(cuts))
        loudness = loudness * jnp.repeat(jnp.exp(steps), extent[dim] // shards_of).reshape((-1,) + (1,) * (len(extent) - 1 - dim))
    return loudness


def normal_values(key, dims, scale, bound, pieces=(), kind=jnp.bfloat16):
    gain = block_levels(key, dims, pieces, -0.22, 0.18) if pieces else 1.0
    drawn = jax.random.normal(key, dims, jnp.float32) * scale * gain
    return jnp.minimum(jnp.maximum(drawn, -bound), bound).astype(kind)


def setup_inputs(seed: int = 0) -> dict:
    streams_of = jax.random.split(jax.random.key(seed), 5)
    gradients = draw_gradients(jax.random.fold_in(streams_of[4], 71), 0)
    keep_rows = draw_keep_rows(jax.random.fold_in(streams_of[4], 71), 0)
    keep_counts = draw_keep_counts(jax.random.fold_in(streams_of[4], 71), 0)
    momentum = normal_values(streams_of[3], (ROW_TILES, TILE, FF), 0.5, 3.0, ((0, 8), (1, 16)), jnp.float32)
    return dict(gradients=gradients, keep_rows=keep_rows, keep_counts=keep_counts, momentum=momentum)


def cosine_table():
    freq = jnp.arange(TILE, dtype=jnp.float32)[:, None]
    place = jnp.arange(TILE, dtype=jnp.float32)[None, :]
    norming = jnp.where(freq == 0, math.sqrt(1.0 / TILE), math.sqrt(2.0 / TILE))
    return norming * jnp.cos(math.pi * (2.0 * place + 1.0) * freq / (2.0 * TILE))

def reference(gradients, keep_rows, keep_counts, momentum):
    cosine = cosine_table()
    cosine_half = cosine.astype(jnp.bfloat16)
    half_wide = cosine_half.astype(jnp.float32)
    slot_ids = jnp.arange(KMAX, dtype=jnp.int32)
    freq_ids = jnp.arange(TILE, dtype=jnp.int32)

    def one_row(row_index):
        block = lax.dynamic_slice_in_dim(gradients, row_index * TILE, TILE, 1)
        grad_tiles = block.reshape(N_REP, TILE, COL_TILES, TILE).astype(jnp.float32)
        first_pass = jnp.einsum('ricj,vj->ricv', grad_tiles, half_wide).astype(jnp.bfloat16)
        spectra = jnp.einsum('ui,ricv->rcuv', half_wide, first_pass.astype(jnp.float32)).astype(jnp.bfloat16)
        row_ids = lax.dynamic_index_in_dim(keep_rows, row_index, 1, keepdims=False)
        row_counts = lax.dynamic_index_in_dim(keep_counts, row_index, 1, keepdims=False)
        live_slot = slot_ids[None, None, :] < row_counts[:, :, None]
        hits = (row_ids[..., None] == freq_ids) & live_slot[..., None]
        kept_mask = jnp.any(hits, axis=2).astype(jnp.float32)
        summed = lax.optimization_barrier(jnp.sum(spectra.astype(jnp.float32) * kept_mask[..., None], axis=0))
        squares = jnp.sum(summed * summed)
        half_decoded = jnp.einsum('ui,cuv->civ', cosine, summed, precision=lax.Precision.HIGHEST).astype(jnp.bfloat16)
        update = jnp.einsum('civ,vj->icj', half_decoded.astype(jnp.float32), half_wide)
        return (update.reshape(TILE, FF), squares)
    update, squares = lax.map(one_row, jnp.arange(ROW_TILES, dtype=jnp.int32))
    energy = jnp.sum(squares)
    shrink = jnp.minimum(1.0, math.sqrt(ROWS * FF) / jnp.sqrt(energy))
    return 0.9 * momentum + shrink * update
```

```python
import functools
import math

import jax
import jax.numpy as jnp
import numpy as np
from jax import lax
from jax.experimental import pallas as pl
from jax.experimental.pallas import tpu as pltpu
from jax.sharding import PartitionSpec as P

TILE = 128
KMAX = 32
REPS = 8
SHARDS = 16
ROW_TILES = 16
OWNED = ROW_TILES // REPS
CHUNKS = (1, 4, 4, 4, 4, 4, 4, 3, 1)
AHEAD = 2
MESH = pl.DeviceIdType.MESH


def cosine_table():
    freq = np.arange(TILE, dtype=np.float64)[:, None]
    place = np.arange(TILE, dtype=np.float64)[None, :]
    norming = np.where(freq == 0, math.sqrt(1.0 / TILE), math.sqrt(2.0 / TILE))
    return norming * np.cos(math.pi * (2.0 * place + 1.0) * freq / (2.0 * TILE))


def dot(a, b, dims=((1,), (0,))):
    return lax.dot_general(a, b, (dims, ((), ())), preferred_element_type=jnp.float32)


def exchange_kernel(
    cols, grads, labels, table, table_t, update, energy_out,
    x_buf, send_buf, recv_buf, upd_buf, lab_mine, lab_send, lab_recv, lab_own, energy,
    energy_a, energy_b,
    x_sem, blk_recv, blk_send, lab_sem, upd_sem, en_sem,
):
    shard = lax.axis_index("shard")
    rep = lax.axis_index("rep")
    starts = [sum(CHUNKS[:k]) for k in range(len(CHUNKS))]
    rep_peers = [lax.rem(rep + j, REPS) for j in range(1, REPS)]
    shard_peers = [lax.rem(shard + j, SHARDS) for j in range(1, SHARDS)]

    def x_copy(k):
        span = pl.ds(starts[k] * TILE, CHUNKS[k] * TILE)
        return pltpu.make_async_copy(grads.at[:, span], x_buf.at[:, span], x_sem.at[k])

    for k in range(len(CHUNKS)):
        x_copy(k).start()

    barrier = pltpu.get_barrier_semaphore()
    for peer in rep_peers:
        pl.semaphore_signal(barrier, inc=1, device_id=(shard, peer), device_id_type=MESH)
    for peer in shard_peers:
        pl.semaphore_signal(barrier, inc=1, device_id=(peer, rep), device_id_type=MESH)

    lab_mine[...] = jnp.zeros_like(lab_mine)
    for group in range(4):
        row = jnp.concatenate([labels[4 * group + t] for t in range(4)], axis=1)
        lab_mine[group, 0:cols] = row
        lab_send[group] = lab_mine[group].astype(jnp.bfloat16)
    energy[...] = jnp.zeros_like(energy)

    pl.semaphore_wait(barrier, REPS + SHARDS - 2)

    def lab_copy(peer):
        return pltpu.make_async_remote_copy(
            src_ref=lab_send.at[peer // 2], dst_ref=lab_recv.at[rep],
            send_sem=lab_sem.at[0], recv_sem=lab_sem.at[1],
            device_id=(shard, peer), device_id_type=MESH)

    for peer in rep_peers:
        lab_copy(peer).start()
    pltpu.make_async_copy(lab_send.at[rep // 2], lab_recv.at[rep], lab_sem.at[1]).start()

    freq = lax.broadcasted_iota(jnp.int32, (TILE, TILE), 0) + 1

    def hits(row):
        return jnp.where(freq == row, 1.0, 0.0).astype(jnp.bfloat16)

    def encode(k):
        x_copy(k).wait()

        def column(c, carry):
            span = pl.ds(pl.multiple_of(c * TILE, TILE), TILE)
            for group in range(4):
                row = lab_mine[group, pl.ds(c, 1), :]
                left = dot(hits(row), table[...], ((0,), (0,))).astype(jnp.bfloat16)
                parts = []
                for t in range(4):
                    q = 4 * group + t
                    tile = x_buf[q * TILE:(q + 1) * TILE, span]
                    parts.append(dot(left[t * KMAX:(t + 1) * KMAX], tile))
                half = jnp.concatenate(parts, axis=0).astype(jnp.bfloat16)
                kept = dot(half, table_t[...]).astype(jnp.bfloat16)
                send_buf[2 * group, c] = kept[:2 * KMAX]
                send_buf[2 * group + 1, c] = kept[2 * KMAX:]
            return carry

        lax.fori_loop(starts[k], starts[k] + CHUNKS[k], column, 0)

    def send_blocks(k):
        span = pl.ds(starts[k], CHUNKS[k])
        for peer in rep_peers:
            pltpu.make_async_remote_copy(
                src_ref=send_buf.at[peer, span], dst_ref=recv_buf.at[rep, span],
                send_sem=blk_send.at[0], recv_sem=blk_recv.at[k],
                device_id=(shard, peer), device_id_type=MESH).start()
        pltpu.make_async_copy(send_buf.at[rep, span], recv_buf.at[rep, span], blk_recv.at[k]).start()

    def own_labels():
        pltpu.make_async_copy(lab_recv, lab_recv, lab_sem.at[1]).wait()
        slot = lax.broadcasted_iota(jnp.int32, lab_send.shape[1:], 1) // KMAX
        for q in range(OWNED):
            for half in range(2):
                total = jnp.zeros(lab_send.shape[1:], jnp.float32)
                for i in range(4):
                    got = lab_recv[4 * half + i].astype(jnp.float32)
                    shift = lax.rem(4 + i - (lax.rem(rep, 2) * 2 + q), 4) * KMAX
                    total += jnp.where(slot == i, pltpu.roll(got, shift, 1), 0.0)
                lab_own[q, half] = total.astype(jnp.int32)

    def decode(k):
        span = pl.ds(starts[k], CHUNKS[k])
        pltpu.make_async_copy(recv_buf.at[:, span], recv_buf.at[:, span], blk_recv.at[k]).wait()

        def column(c, carry):
            outs = []
            for q in range(OWNED):
                places = jnp.concatenate(
                    [hits(lab_own[q, half, pl.ds(c, 1), :]) for half in range(2)], axis=1)
                block = recv_buf[:, c, q * KMAX:(q + 1) * KMAX, :].reshape(REPS * KMAX, TILE)
                summed = dot(places, block)
                energy[...] += jnp.sum((summed * summed).reshape(TILE // 8, 8, TILE), axis=0)
                rows = dot(table_t[...], summed.astype(jnp.bfloat16)).astype(jnp.bfloat16)
                outs.append(dot(rows, table[...]).reshape(SHARDS, TILE // SHARDS, TILE))
            both = jnp.concatenate(outs, axis=1).astype(jnp.bfloat16)
            upd_buf[:, :, pl.ds(pl.multiple_of(c * TILE, TILE), TILE)] = both
            return carry

        lax.fori_loop(starts[k], starts[k] + CHUNKS[k], column, 0)

    def send_update(k):
        width = CHUNKS[k] * TILE
        src = pl.ds(starts[k] * TILE, width)
        dst = pl.ds(pl.multiple_of((shard * cols + starts[k]) * TILE, TILE), width)
        for peer in shard_peers:
            pltpu.make_async_remote_copy(
                src_ref=upd_buf.at[peer, :, src], dst_ref=update.at[:, dst],
                send_sem=upd_sem.at[0], recv_sem=upd_sem.at[1],
                device_id=(peer, rep), device_id_type=MESH).start()
        pltpu.make_async_copy(upd_buf.at[shard, :, src], update.at[:, dst], upd_sem.at[1]).start()

    last = len(CHUNKS)
    for k in range(AHEAD):
        encode(k)
        send_blocks(k)
    own_labels()
    for k in range(last):
        if k + AHEAD < last:
            encode(k + AHEAD)
            send_blocks(k + AHEAD)
        decode(k)
        send_update(k)

    energy_a[shard] = energy[...]
    for peer in shard_peers:
        pltpu.make_async_remote_copy(
            src_ref=energy, dst_ref=energy_a.at[shard],
            send_sem=en_sem.at[0], recv_sem=en_sem.at[1],
            device_id=(peer, rep), device_id_type=MESH).start()
    others = energy_a.at[pl.ds(0, SHARDS - 1)]
    pltpu.make_async_copy(others, others, en_sem.at[1]).wait()
    pltpu.make_async_copy(others, others, en_sem.at[0]).wait()
    energy[...] = jnp.sum(energy_a[...], axis=0)
    energy_b[rep] = energy[...]
    for peer in rep_peers:
        pltpu.make_async_remote_copy(
            src_ref=energy, dst_ref=energy_b.at[rep],
            send_sem=en_sem.at[2], recv_sem=en_sem.at[3],
            device_id=(shard, peer), device_id_type=MESH).start()
    others = energy_b.at[pl.ds(0, REPS - 1)]
    pltpu.make_async_copy(others, others, en_sem.at[3]).wait()
    energy_out[...] = jnp.sum(energy_b[...], axis=0)
    pltpu.make_async_copy(others, others, en_sem.at[2]).wait()

    sent = send_buf.at[pl.ds(0, REPS - 1)]
    pltpu.make_async_copy(sent, sent, blk_send.at[0]).wait()
    sent = lab_recv.at[pl.ds(0, REPS - 1)]
    pltpu.make_async_copy(sent, sent, lab_sem.at[0]).wait()
    sent = upd_buf.at[pl.ds(0, SHARDS - 1)]
    pltpu.make_async_copy(sent, sent, upd_sem.at[0]).wait()
    pltpu.make_async_copy(upd_buf, upd_buf, upd_sem.at[1]).wait()


def step_kernel(limit, momentum, update, energy, out):
    total = jnp.sum(energy[...], keepdims=True)
    shrink = jnp.minimum(1.0, limit / jnp.sqrt(total))
    rows = update[...].astype(jnp.float32).reshape(momentum.shape)
    out[...] = 0.9 * momentum[...] + shrink * rows


def body(gradients, keep_rows, keep_counts, momentum):
    _, all_rows, width = gradients.shape
    cols = width // TILE
    assert sum(CHUNKS) == cols
    cols_pad = -(-cols // 16) * 16
    cosine = cosine_table().astype(np.float32)
    table = jnp.asarray(cosine).astype(jnp.bfloat16)
    table_t = jnp.asarray(np.ascontiguousarray(cosine.T)).astype(jnp.bfloat16)
    live = jnp.arange(KMAX, dtype=jnp.int32) < keep_counts[0][:, :, None]
    labels = jnp.where(live, keep_rows[0] + 1, 0)
    full = SHARDS * width
    vmem = pl.BlockSpec(memory_space=pltpu.VMEM)
    anywhere = pl.BlockSpec(memory_space=pl.ANY)
    block = (REPS, cols, OWNED * KMAX, TILE)
    part = OWNED * TILE // SHARDS
    update, energy = pl.pallas_call(
        functools.partial(exchange_kernel, cols),
        out_shape=(
            jax.ShapeDtypeStruct((part, full), jnp.bfloat16),
            jax.ShapeDtypeStruct((8, TILE), jnp.float32),
        ),
        in_specs=[anywhere, vmem, vmem, vmem],
        out_specs=(anywhere, vmem),
        scratch_shapes=[
            pltpu.VMEM((all_rows, width), jnp.bfloat16),
            pltpu.VMEM(block, jnp.bfloat16),
            pltpu.VMEM(block, jnp.bfloat16),
            pltpu.VMEM((SHARDS, part, width), jnp.bfloat16),
            pltpu.VMEM((4, cols_pad, TILE), jnp.int32),
            pltpu.VMEM((4, cols_pad, TILE), jnp.bfloat16),
            pltpu.VMEM((REPS, cols_pad, TILE), jnp.bfloat16),
            pltpu.VMEM((OWNED, 2, cols_pad, TILE), jnp.int32),
            pltpu.VMEM((8, TILE), jnp.float32),
            pltpu.VMEM((SHARDS, 8, TILE), jnp.float32),
            pltpu.VMEM((REPS, 8, TILE), jnp.float32),
            pltpu.SemaphoreType.DMA((len(CHUNKS),)),
            pltpu.SemaphoreType.DMA((len(CHUNKS),)),
            pltpu.SemaphoreType.DMA((1,)),
            pltpu.SemaphoreType.DMA((2,)),
            pltpu.SemaphoreType.DMA((2,)),
            pltpu.SemaphoreType.DMA((4,)),
        ],
        compiler_params=pltpu.CompilerParams(
            collective_id=0, has_side_effects=True, vmem_limit_bytes=48 * 1024 * 1024),
    )(gradients[0], labels, table, table_t)

    limit = math.sqrt(all_rows * full)
    steps = 8
    wide = full // steps
    return pl.pallas_call(
        functools.partial(step_kernel, limit),
        grid=(steps,),
        out_shape=jax.ShapeDtypeStruct(momentum.shape, momentum.dtype),
        in_specs=[
            pl.BlockSpec((OWNED, part // OWNED, wide), lambda i: (0, 0, i)),
            pl.BlockSpec((part, wide), lambda i: (0, i)),
            pl.BlockSpec((8, TILE), lambda i: (0, 0)),
        ],
        out_specs=pl.BlockSpec((OWNED, part // OWNED, wide), lambda i: (0, 0, i)),
        compiler_params=pltpu.CompilerParams(vmem_limit_bytes=16 * 1024 * 1024),
    )(momentum, update, energy)


def solution(mesh):
    return jax.shard_map(
        body,
        mesh=mesh,
        in_specs=(
            P("rep", None, "shard"),
            P("rep", None, "shard", None),
            P("rep", None, "shard"),
            P("rep", "shard", None),
        ),
        out_specs=P("rep", "shard", None),
        check_vma=False,
    )
```

```python
import functools
import math

import jax
import jax.numpy as jnp
import numpy as np
from jax import lax
from jax.experimental import pallas as pl
from jax.experimental.pallas import tpu as pltpu
from jax.sharding import PartitionSpec as P

TILE = 128
KMAX = 32
REPS = 8
SHARDS = 16
ROW_TILES = 16
OWNED = ROW_TILES // REPS
CHUNKS = (1, 2, 4, 4, 4, 4, 4, 4, 2)
AHEAD = 2
EARLY = 1
PAIR = 2
MESH = pl.DeviceIdType.MESH


def cosine_table():
    freq = np.arange(TILE, dtype=np.float64)[:, None]
    place = np.arange(TILE, dtype=np.float64)[None, :]
    norming = np.where(freq == 0, math.sqrt(1.0 / TILE), math.sqrt(2.0 / TILE))
    return norming * np.cos(math.pi * (2.0 * place + 1.0) * freq / (2.0 * TILE))


def dot(a, b, dims=((1,), (0,))):
    return lax.dot_general(a, b, (dims, ((), ())), preferred_element_type=jnp.float32)


def exchange_kernel(
    cols, grads, keep_rows, keep_counts, tables, update, energy_out,
    x_buf, send_buf, recv_buf, upd_buf, rows_buf, counts_buf, tables_buf,
    lab_wide, lab_mine, lab_send, lab_recv, lab_own, energy, energy_row, energy_a, energy_b,
    x_sem, in_sem, blk_recv, blk_send, lab_sem, upd_sem, en_sem, ready,
):
    shard = lax.axis_index("shard")
    rep = lax.axis_index("rep")
    starts = [sum(CHUNKS[:k]) for k in range(len(CHUNKS))]
    rep_peers = [lax.rem(rep // 2 + y, 4) * 2 + lax.rem(rep + core, 2)
                 for y in (2, 1, 3, 0) for core in (0, 1) if y or core]
    hops = sorted(((z, x) for z in range(4) for x in range(4) if z or x), key=lambda p: -(2 - abs(p[0] - 2)) - (2 - abs(p[1] - 2)))
    ring = [lax.rem(shard // 4 + z, 4) * 4 + lax.rem(shard + x, 4) for z, x in hops]
    shard_peers = ring
    near = [peer for peer, (z, x) in zip(ring, hops) if not (z and x)]
    along_z = [peer for peer, (z, x) in zip(ring, hops) if not x]

    def x_copy(k):
        span = pl.ds(starts[k] * TILE, CHUNKS[k] * TILE)
        return pltpu.make_async_copy(grads.at[:, span], x_buf.at[:, span], x_sem.at[k])

    small = [
        pltpu.make_async_copy(keep_rows, rows_buf, in_sem.at[0]),
        pltpu.make_async_copy(keep_counts, counts_buf, in_sem.at[1]),
        pltpu.make_async_copy(tables, tables_buf, in_sem.at[2]),
    ]
    barrier = pltpu.get_barrier_semaphore()
    for copy in small:
        copy.start()
    x_copy(0).start()
    for peer in rep_peers:
        pl.semaphore_signal(barrier, inc=1, device_id=(shard, peer), device_id_type=MESH)
    for peer in near:
        pl.semaphore_signal(barrier, inc=1, device_id=(peer, rep), device_id_type=MESH)
    for k in range(1, len(CHUNKS)):
        x_copy(k).start()

    energy[...] = jnp.zeros_like(energy)
    for copy in small:
        copy.wait()
    table = tables_buf.at[0]
    table_t = tables_buf.at[1]

    for c in range(cols):
        live = lax.broadcasted_iota(jnp.int32, (ROW_TILES, KMAX), 1) < counts_buf[:, c:c + 1]
        wide = jnp.where(live, rows_buf[c] + 1, 0)
        lab_wide[c * ROW_TILES:(c + 1) * ROW_TILES] = jnp.concatenate([wide] * 4, axis=1)
    slot = lax.broadcasted_iota(jnp.int32, (cols, TILE), 1) // KMAX
    lab_mine[...] = jnp.zeros_like(lab_mine)
    for group in range(4):
        row = jnp.zeros((cols, TILE), jnp.int32)
        for t in range(4):
            got = lab_wide[pl.ds(4 * group + t, cols, stride=ROW_TILES), :]
            row = jnp.where(slot == t, got, row)
        lab_mine[group, 0:cols] = row
        lab_send[group] = lab_mine[group].astype(jnp.bfloat16)

    def lab_copy(peer):
        return pltpu.make_async_remote_copy(
            src_ref=lab_send.at[peer // 2], dst_ref=lab_recv.at[rep],
            send_sem=lab_sem.at[0], recv_sem=lab_sem.at[1],
            device_id=(shard, peer), device_id_type=MESH)

    freq = lax.broadcasted_iota(jnp.int32, (TILE, TILE), 0) + 1

    def hits(row):
        return jnp.where(freq == row, 1.0, 0.0).astype(jnp.bfloat16)

    def encode(k):
        x_copy(k).wait()
        pair = min(PAIR, CHUNKS[k])

        def columns(step, carry):
            first = starts[k] + step * pair
            span = pl.ds(pl.multiple_of(first * TILE, TILE), pair * TILE)
            picks = [hits(lab_mine[group, pl.ds(first + i, 1), :]) for i in range(pair) for group in range(4)]
            left = dot(jnp.concatenate(picks, axis=1), table[...], ((0,), (0,))).astype(jnp.bfloat16)
            parts = [[None] * ROW_TILES for _ in range(pair)]
            for q in range(ROW_TILES):
                rows = [left[(i * ROW_TILES + q) * KMAX:(i * ROW_TILES + q + 1) * KMAX] for i in range(pair)]
                both = dot(jnp.concatenate(rows, axis=0), x_buf[q * TILE:(q + 1) * TILE, span])
                for i in range(pair):
                    parts[i][q] = both[i * KMAX:(i + 1) * KMAX, i * TILE:(i + 1) * TILE].astype(jnp.bfloat16)
            half = jnp.concatenate(parts[0] + (parts[1] if pair > 1 else []), axis=0)
            kept = dot(half, table_t[...]).astype(jnp.bfloat16)
            for i in range(pair):
                for peer in range(REPS):
                    at = (i * REPS + peer) * OWNED * KMAX
                    send_buf[peer, first + i] = kept[at:at + OWNED * KMAX]
            return carry

        lax.fori_loop(0, CHUNKS[k] // pair, columns, 0)

    def send_blocks(k):
        span = pl.ds(starts[k], CHUNKS[k])
        for peer in rep_peers:
            pltpu.make_async_remote_copy(
                src_ref=send_buf.at[peer, span], dst_ref=recv_buf.at[rep, span],
                send_sem=blk_send.at[0], recv_sem=blk_recv.at[k],
                device_id=(shard, peer), device_id_type=MESH).start()
        pltpu.make_async_copy(send_buf.at[rep, span], recv_buf.at[rep, span], blk_recv.at[k]).start()

    def own_labels():
        pltpu.make_async_copy(lab_recv, lab_recv, lab_sem.at[1]).wait()
        slot = lax.broadcasted_iota(jnp.int32, lab_send.shape[1:], 1) // KMAX
        for q in range(OWNED):
            for half in range(2):
                total = jnp.zeros(lab_send.shape[1:], jnp.float32)
                for i in range(4):
                    got = lab_recv[4 * half + i].astype(jnp.float32)
                    shift = lax.rem(4 + i - (lax.rem(rep, 2) * 2 + q), 4) * KMAX
                    total += jnp.where(slot == i, pltpu.roll(got, shift, 1), 0.0)
                lab_own[q, half] = total.astype(jnp.int32)

    def decode(k):
        span = pl.ds(starts[k], CHUNKS[k])
        pltpu.make_async_copy(recv_buf.at[:, span], recv_buf.at[:, span], blk_recv.at[k]).wait()

        pair = min(PAIR, CHUNKS[k])

        def columns(step, carry):
            first = starts[k] + step * pair
            sums = []
            for i in range(pair):
                for q in range(OWNED):
                    places = jnp.concatenate(
                        [hits(lab_own[q, half, pl.ds(first + i, 1), :]) for half in range(2)], axis=1)
                    block = recv_buf[:, first + i, q * KMAX:(q + 1) * KMAX, :].reshape(REPS * KMAX, TILE)
                    sums.append(dot(places, block))
            squares = sum(jnp.sum((v * v).reshape(TILE // 8, 8, TILE), axis=0) for v in sums)
            energy[...] += squares
            wide = jnp.concatenate([v.astype(jnp.bfloat16) for v in sums], axis=1)
            rows = dot(table_t[...], wide).astype(jnp.bfloat16)
            tall = jnp.concatenate([rows[:, n * TILE:(n + 1) * TILE] for n in range(len(sums))], axis=0)
            done = dot(tall, table[...]).reshape(len(sums), SHARDS, TILE // SHARDS, TILE)
            for i in range(pair):
                both = jnp.concatenate([done[i * OWNED + q] for q in range(OWNED)], axis=1).astype(jnp.bfloat16)
                upd_buf[:, :, pl.ds(pl.multiple_of((first + i) * TILE, TILE), TILE)] = both
            return carry

        lax.fori_loop(0, CHUNKS[k] // pair, columns, 0)

    def send_update(k):
        width = CHUNKS[k] * TILE
        src = pl.ds(starts[k] * TILE, width)
        dst = pl.ds(pl.multiple_of((shard * cols + starts[k]) * TILE, TILE), width)
        for peer in shard_peers:
            pltpu.make_async_remote_copy(
                src_ref=upd_buf.at[peer, :, src], dst_ref=update.at[:, dst],
                send_sem=upd_sem.at[0], recv_sem=upd_sem.at[1],
                device_id=(peer, rep), device_id_type=MESH).start()
        pltpu.make_async_copy(upd_buf.at[shard, :, src], update.at[:, dst], upd_sem.at[1]).start()

    last = len(CHUNKS)
    for k in range(EARLY):
        encode(k)
    pl.semaphore_wait(barrier, REPS - 1 + len(near))
    send_blocks(0)
    for peer in rep_peers:
        lab_copy(peer).start()
    pltpu.make_async_copy(lab_send.at[rep // 2], lab_recv.at[rep], lab_sem.at[1]).start()
    for peer in along_z:
        pl.semaphore_signal(ready, inc=1, device_id=(peer, rep), device_id_type=MESH)
    for k in range(1, EARLY):
        send_blocks(k)
    for k in range(EARLY, AHEAD):
        encode(k)
        send_blocks(k)
    for k in range(last):
        if k + AHEAD < last:
            encode(k + AHEAD)
            send_blocks(k + AHEAD)
        if k == 0:
            own_labels()
        decode(k)
        if k == 0:
            pl.semaphore_wait(ready, len(along_z))
        send_update(k)

    sent = send_buf.at[pl.ds(0, REPS - 1)]
    pltpu.make_async_copy(sent, sent, blk_send.at[0]).wait()
    energy_row[0] = jnp.sum(energy[...], axis=0, keepdims=True)
    energy_a[shard] = energy_row[0]
    for peer in shard_peers:
        pltpu.make_async_remote_copy(
            src_ref=energy_row.at[0], dst_ref=energy_a.at[shard],
            send_sem=en_sem.at[0], recv_sem=en_sem.at[1],
            device_id=(peer, rep), device_id_type=MESH).start()
    sent = lab_recv.at[pl.ds(0, REPS - 1)]
    pltpu.make_async_copy(sent, sent, lab_sem.at[0]).wait()
    others = energy_a.at[pl.ds(0, SHARDS - 1)]
    pltpu.make_async_copy(others, others, en_sem.at[1]).wait()
    energy_row[1] = jnp.sum(energy_a[...], axis=0)
    energy_b[rep] = energy_row[1]
    for peer in rep_peers:
        pltpu.make_async_remote_copy(
            src_ref=energy_row.at[1], dst_ref=energy_b.at[rep],
            send_sem=en_sem.at[2], recv_sem=en_sem.at[3],
            device_id=(shard, peer), device_id_type=MESH).start()
    pltpu.make_async_copy(others, others, en_sem.at[0]).wait()
    sent = upd_buf.at[pl.ds(0, SHARDS - 1)]
    pltpu.make_async_copy(sent, sent, upd_sem.at[0]).wait()
    pltpu.make_async_copy(upd_buf, upd_buf, upd_sem.at[1]).wait()
    others = energy_b.at[pl.ds(0, REPS - 1)]
    pltpu.make_async_copy(others, others, en_sem.at[3]).wait()
    energy_out[...] = jnp.sum(energy_b[...], axis=0)
    pltpu.make_async_copy(others, others, en_sem.at[2]).wait()


def step_kernel(limit, momentum, update, energy, out, out_buf, sems):
    total = jnp.sum(energy[...], keepdims=True)
    shrink = jnp.minimum(1.0, limit / jnp.sqrt(total))
    steps = sems.shape[0]
    wide = momentum.shape[2] // steps
    copies = []
    for i in range(steps):
        span = pl.ds(i * wide, wide)
        rows = update[:, span].astype(jnp.float32)
        for q in range(OWNED):
            height = momentum.shape[1]
            out_buf[q, :, span] = 0.9 * momentum[q, :, span] + shrink * rows[q * height:(q + 1) * height]
        copies.append(pltpu.make_async_copy(out_buf.at[:, :, span], out.at[:, :, span], sems.at[i]))
        copies[-1].start()
    for copy in copies:
        copy.wait()


def body(gradients, keep_rows, keep_counts, momentum):
    _, all_rows, width = gradients.shape
    cols = width // TILE
    assert sum(CHUNKS) == cols
    cols_pad = -(-cols // 16) * 16
    cosine = cosine_table().astype(np.float32)
    tables = jnp.asarray(np.stack([cosine, cosine.T])).astype(jnp.bfloat16)
    full = SHARDS * width
    vmem = pl.BlockSpec(memory_space=pltpu.VMEM)
    anywhere = pl.BlockSpec(memory_space=pl.ANY)
    block = (REPS, cols, OWNED * KMAX, TILE)
    part = OWNED * TILE // SHARDS
    update, energy = pl.pallas_call(
        functools.partial(exchange_kernel, cols),
        out_shape=(
            jax.ShapeDtypeStruct((part, full), jnp.bfloat16),
            jax.ShapeDtypeStruct((1, TILE), jnp.float32),
        ),
        in_specs=[pl.BlockSpec(memory_space=pltpu.HBM)] * 4,
        out_specs=(anywhere, vmem),
        scratch_shapes=[
            pltpu.VMEM((all_rows, width), jnp.bfloat16),
            pltpu.VMEM(block, jnp.bfloat16),
            pltpu.VMEM(block, jnp.bfloat16),
            pltpu.VMEM((SHARDS, part, width), jnp.bfloat16),
            pltpu.VMEM((cols, ROW_TILES, KMAX), jnp.int32),
            pltpu.VMEM((ROW_TILES, cols), jnp.int32),
            pltpu.VMEM((2, TILE, TILE), jnp.bfloat16),
            pltpu.VMEM((cols * ROW_TILES, TILE), jnp.int32),
            pltpu.VMEM((4, cols_pad, TILE), jnp.int32),
            pltpu.VMEM((4, cols_pad, TILE), jnp.bfloat16),
            pltpu.VMEM((REPS, cols_pad, TILE), jnp.bfloat16),
            pltpu.VMEM((OWNED, 2, cols_pad, TILE), jnp.int32),
            pltpu.VMEM((8, TILE), jnp.float32),
            pltpu.VMEM((2, 1, TILE), jnp.float32),
            pltpu.VMEM((SHARDS, 1, TILE), jnp.float32),
            pltpu.VMEM((REPS, 1, TILE), jnp.float32),
            pltpu.SemaphoreType.DMA((len(CHUNKS),)),
            pltpu.SemaphoreType.DMA((3,)),
            pltpu.SemaphoreType.DMA((len(CHUNKS),)),
            pltpu.SemaphoreType.DMA((1,)),
            pltpu.SemaphoreType.DMA((2,)),
            pltpu.SemaphoreType.DMA((2,)),
            pltpu.SemaphoreType.DMA((4,)),
            pltpu.SemaphoreType.REGULAR,
        ],
        compiler_params=pltpu.CompilerParams(
            collective_id=0, has_side_effects=True, vmem_limit_bytes=48 * 1024 * 1024),
    )(gradients[0], jnp.transpose(keep_rows[0], (1, 0, 2)), keep_counts[0], tables)

    limit = math.sqrt(all_rows * full)
    return pl.pallas_call(
        functools.partial(step_kernel, limit),
        out_shape=jax.ShapeDtypeStruct(momentum.shape, momentum.dtype),
        in_specs=[vmem, vmem, vmem],
        out_specs=anywhere,
        scratch_shapes=[pltpu.VMEM(momentum.shape, jnp.float32), pltpu.SemaphoreType.DMA((8,))],
        compiler_params=pltpu.CompilerParams(vmem_limit_bytes=16 * 1024 * 1024),
    )(momentum, update, energy)


def solution(mesh):
    return jax.shard_map(
        body,
        mesh=mesh,
        in_specs=(
            P("rep", None, "shard"),
            P("rep", None, "shard", None),
            P("rep", None, "shard"),
            P("rep", "shard", None),
        ),
        out_specs=P("rep", "shard", None),
        check_vma=False,
    )
```

```python
import functools
import math

import jax
import jax.numpy as jnp
import numpy as np
from jax import lax
from jax.experimental import pallas as pl
from jax.experimental.pallas import tpu as pltpu
from jax.sharding import PartitionSpec as P

TILE = 128
KMAX = 32
REPS = 8
SHARDS = 16
ROW_TILES = 16
OWNED = ROW_TILES // REPS
CHUNKS = (1, 2, 4, 4, 4, 4, 4, 2, 2, 1, 1)
AHEAD = 3
PAIR = 2
MESH = pl.DeviceIdType.MESH


def cosine_table():
    freq = np.arange(TILE, dtype=np.float64)[:, None]
    place = np.arange(TILE, dtype=np.float64)[None, :]
    norming = np.where(freq == 0, math.sqrt(1.0 / TILE), math.sqrt(2.0 / TILE))
    return norming * np.cos(math.pi * (2.0 * place + 1.0) * freq / (2.0 * TILE))


def dot(a, b, dims=((1,), (0,))):
    return lax.dot_general(a, b, (dims, ((), ())), preferred_element_type=jnp.float32)


def exchange_kernel(
    cols, grads, keep_rows, keep_counts, tables, update, energy_out,
    x_buf, send_buf, recv_buf, upd_buf, rows_buf, counts_buf, tables_buf,
    lab_wide, lab_mine, lab_send, lab_recv, lab_own, energy, energy_row, energy_a, energy_b,
    x_sem, in_sem, blk_recv, blk_send, lab_sem, upd_sem, en_sem, ready,
):
    shard = lax.axis_index("shard")
    rep = lax.axis_index("rep")
    starts = [sum(CHUNKS[:k]) for k in range(len(CHUNKS))]
    rep_peers = [lax.rem(rep // 2 + y, 4) * 2 + lax.rem(rep + core, 2)
                 for y in (2, 1, 3, 0) for core in (0, 1) if y or core]
    hops = sorted(((z, x) for z in range(4) for x in range(4) if z or x), key=lambda p: -(2 - abs(p[0] - 2)) - (2 - abs(p[1] - 2)))
    ring = [lax.rem(shard // 4 + z, 4) * 4 + lax.rem(shard + x, 4) for z, x in hops]
    shard_peers = [j + (j >= shard).astype(jnp.int32) for j in range(SHARDS - 1)]
    near = [peer for peer, (z, x) in zip(ring, hops) if not (z and x)]
    along_z = [peer for peer, (z, x) in zip(ring, hops) if not x]

    def x_copy(k):
        span = pl.ds(starts[k] * TILE, CHUNKS[k] * TILE)
        return pltpu.make_async_copy(grads.at[:, span], x_buf.at[:, span], x_sem.at[k])

    small = [
        pltpu.make_async_copy(keep_rows, rows_buf, in_sem.at[0]),
        pltpu.make_async_copy(keep_counts, counts_buf, in_sem.at[1]),
        pltpu.make_async_copy(tables, tables_buf, in_sem.at[2]),
    ]
    barrier = pltpu.get_barrier_semaphore()
    for peer in rep_peers:
        pl.semaphore_signal(barrier, inc=1, device_id=(shard, peer), device_id_type=MESH)
    for peer in near:
        pl.semaphore_signal(barrier, inc=1, device_id=(peer, rep), device_id_type=MESH)
    for copy in small:
        copy.start()
    x_copy(0).start()
    for k in range(1, len(CHUNKS)):
        x_copy(k).start()

    energy[...] = jnp.zeros_like(energy)
    for copy in small:
        copy.wait()
    table = tables_buf.at[0]
    table_t = tables_buf.at[1]

    def own_rows(first, count):
        for c in range(first, first + count):
            live = lax.broadcasted_iota(jnp.int32, (ROW_TILES, KMAX), 1) < counts_buf[:, c:c + 1]
            wide = jnp.where(live, rows_buf[c] + 1, 0)
            lab_wide[c * ROW_TILES:(c + 1) * ROW_TILES] = jnp.concatenate([wide] * 4, axis=1)
        slot = lax.broadcasted_iota(jnp.int32, (count, TILE), 1) // KMAX
        for group in range(4):
            row = jnp.zeros((count, TILE), jnp.int32)
            for t in range(4):
                got = lab_wide[pl.ds(first * ROW_TILES + 4 * group + t, count, stride=ROW_TILES), :]
                row = jnp.where(slot == t, got, row)
            lab_mine[group, first:first + count] = row

    def pack_rows():
        half = lab_send.shape[1]
        lower = lax.broadcasted_iota(jnp.int32, (half, TILE), 1) < TILE // 2
        for group in range(4):
            early, late = lab_mine[group, 0:half], lab_mine[group, half:2 * half]
            lab_send[2 * group] = jnp.where(lower, early, pltpu.roll(late, TILE // 2, 1)).astype(jnp.bfloat16)
            lab_send[2 * group + 1] = jnp.where(lower, pltpu.roll(early, TILE // 2, 1), late).astype(jnp.bfloat16)

    lab_mine[...] = jnp.zeros_like(lab_mine)
    own_rows(0, 1)

    def lab_copy(peer):
        return pltpu.make_async_remote_copy(
            src_ref=lab_send.at[peer], dst_ref=lab_recv.at[rep],
            send_sem=lab_sem.at[0], recv_sem=lab_sem.at[1],
            device_id=(shard, peer), device_id_type=MESH)

    freq = lax.broadcasted_iota(jnp.int32, (TILE, TILE), 0) + 1

    def hits(row):
        return jnp.where(freq == row, 1.0, 0.0).astype(jnp.bfloat16)

    def encode(k):
        x_copy(k).wait()
        pair = min(PAIR, CHUNKS[k])

        def columns(step, carry):
            first = starts[k] + step * pair
            span = pl.ds(pl.multiple_of(first * TILE, TILE), pair * TILE)
            picks = [hits(lab_mine[group, pl.ds(first + i, 1), :]) for i in range(pair) for group in range(4)]
            left = dot(jnp.concatenate(picks, axis=1), table[...], ((0,), (0,))).astype(jnp.bfloat16)
            parts = [[None] * ROW_TILES for _ in range(pair)]
            for q in range(ROW_TILES):
                rows = [left[(i * ROW_TILES + q) * KMAX:(i * ROW_TILES + q + 1) * KMAX] for i in range(pair)]
                both = dot(jnp.concatenate(rows, axis=0), x_buf[q * TILE:(q + 1) * TILE, span])
                for i in range(pair):
                    parts[i][q] = both[i * KMAX:(i + 1) * KMAX, i * TILE:(i + 1) * TILE].astype(jnp.bfloat16)
            half = jnp.concatenate(parts[0] + (parts[1] if pair > 1 else []), axis=0)
            kept = dot(half, table_t[...]).astype(jnp.bfloat16)
            for i in range(pair):
                for peer in range(REPS):
                    at = (i * REPS + peer) * OWNED * KMAX
                    send_buf[peer, first + i] = kept[at:at + OWNED * KMAX]
            return carry

        lax.fori_loop(0, CHUNKS[k] // pair, columns, 0)

    def send_blocks(k):
        span = pl.ds(starts[k], CHUNKS[k])
        for peer in rep_peers:
            pltpu.make_async_remote_copy(
                src_ref=send_buf.at[peer, span], dst_ref=recv_buf.at[rep, span],
                send_sem=blk_send.at[0], recv_sem=blk_recv.at[k],
                device_id=(shard, peer), device_id_type=MESH).start()
        pltpu.make_async_copy(send_buf.at[rep, span], recv_buf.at[rep, span], blk_recv.at[k]).start()

    def own_labels():
        pltpu.make_async_copy(lab_recv, lab_recv, lab_sem.at[1]).wait()
        half = lab_send.shape[1]
        slot = lax.broadcasted_iota(jnp.int32, (half, TILE), 1) // KMAX
        for part in range(2):
            for group in range(2):
                for q in range(OWNED):
                    total = jnp.zeros((half, TILE), jnp.float32)
                    for i in range(4):
                        got = lab_recv[4 * group + i].astype(jnp.float32)
                        shift = (i - q - 2 * part) % 4 * KMAX
                        moved = pltpu.roll(got, shift, 1) if shift else got
                        total = jnp.where(slot == i, moved, total)
                    lab_own[q, group, part * half:(part + 1) * half] = total.astype(jnp.int32)

    def decode(k, summed_up=None):
        span = pl.ds(starts[k], CHUNKS[k])
        pltpu.make_async_copy(recv_buf.at[:, span], recv_buf.at[:, span], blk_recv.at[k]).wait()

        pair = min(PAIR, CHUNKS[k])

        def columns(step, carry):
            first = starts[k] + step * pair
            sums = []
            for i in range(pair):
                for q in range(OWNED):
                    places = jnp.concatenate(
                        [hits(lab_own[q, half, pl.ds(first + i, 1), :]) for half in range(2)], axis=1)
                    block = recv_buf[:, first + i, q * KMAX:(q + 1) * KMAX, :].reshape(REPS * KMAX, TILE)
                    sums.append(dot(places, block))
            squares = sum(jnp.sum((v * v).reshape(TILE // 8, 8, TILE), axis=0) for v in sums)
            energy[...] += squares
            if summed_up is not None:
                summed_up()
            wide = jnp.concatenate([v.astype(jnp.bfloat16) for v in sums], axis=1)
            rows = dot(table_t[...], wide).astype(jnp.bfloat16)
            tall = jnp.concatenate([rows[:, n * TILE:(n + 1) * TILE] for n in range(len(sums))], axis=0)
            done = dot(tall, table[...]).reshape(len(sums), SHARDS, TILE // SHARDS, TILE)
            for i in range(pair):
                both = jnp.concatenate([done[i * OWNED + q] for q in range(OWNED)], axis=1).astype(jnp.bfloat16)
                upd_buf[:, :, pl.ds(pl.multiple_of((first + i) * TILE, TILE), TILE)] = both
            return carry

        if CHUNKS[k] == pair:
            columns(0, 0)
        else:
            lax.fori_loop(0, CHUNKS[k] // pair, columns, 0)

    def send_update(k):
        width = CHUNKS[k] * TILE
        src = pl.ds(starts[k] * TILE, width)
        dst = pl.ds(pl.multiple_of((shard * cols + starts[k]) * TILE, TILE), width)
        for peer in shard_peers:
            pltpu.make_async_remote_copy(
                src_ref=upd_buf.at[peer, :, src], dst_ref=update.at[:, dst],
                send_sem=upd_sem.at[0], recv_sem=upd_sem.at[1],
                device_id=(peer, rep), device_id_type=MESH).start()
        pltpu.make_async_copy(upd_buf.at[shard, :, src], update.at[:, dst], upd_sem.at[1]).start()

    def send_energy():
        energy_row[0] = jnp.sum(energy[...], axis=0, keepdims=True)
        energy_a[shard] = energy_row[0]
        for peer in shard_peers:
            pltpu.make_async_remote_copy(
                src_ref=energy_row.at[0], dst_ref=energy_a.at[shard],
                send_sem=en_sem.at[0], recv_sem=en_sem.at[1],
                device_id=(peer, rep), device_id_type=MESH).start()

    last = len(CHUNKS)
    encode(0)
    pl.semaphore_wait(barrier, REPS - 1 + len(near))
    send_blocks(0)
    own_rows(1, cols - 1)
    encode(1)
    send_blocks(1)
    pack_rows()
    for peer in rep_peers:
        lab_copy(peer).start()
    pltpu.make_async_copy(lab_send.at[rep], lab_recv.at[rep], lab_sem.at[1]).start()
    for peer in along_z:
        pl.semaphore_signal(ready, inc=1, device_id=(peer, rep), device_id_type=MESH)
    for k in range(2, AHEAD):
        encode(k)
        send_blocks(k)
    for k in range(last):
        if k + AHEAD < last:
            encode(k + AHEAD)
            send_blocks(k + AHEAD)
        if k == 0:
            own_labels()
        decode(k, send_energy if k == last - 1 else None)
        if k == 0:
            pl.semaphore_wait(ready, len(along_z))
        send_update(k)

    sent = send_buf.at[pl.ds(0, REPS - 1)]
    pltpu.make_async_copy(sent, sent, blk_send.at[0]).wait()
    sent = lab_recv.at[pl.ds(0, REPS - 1)]
    pltpu.make_async_copy(sent, sent, lab_sem.at[0]).wait()
    others = energy_a.at[pl.ds(0, SHARDS - 1)]
    pltpu.make_async_copy(others, others, en_sem.at[1]).wait()
    energy_row[1] = jnp.sum(energy_a[...], axis=0)
    energy_b[rep] = energy_row[1]
    for peer in rep_peers:
        pltpu.make_async_remote_copy(
            src_ref=energy_row.at[1], dst_ref=energy_b.at[rep],
            send_sem=en_sem.at[2], recv_sem=en_sem.at[3],
            device_id=(shard, peer), device_id_type=MESH).start()
    pltpu.make_async_copy(others, others, en_sem.at[0]).wait()
    sent = upd_buf.at[pl.ds(0, SHARDS - 1)]
    pltpu.make_async_copy(sent, sent, upd_sem.at[0]).wait()
    pltpu.make_async_copy(upd_buf, upd_buf, upd_sem.at[1]).wait()
    others = energy_b.at[pl.ds(0, REPS - 1)]
    pltpu.make_async_copy(others, others, en_sem.at[3]).wait()
    energy_out[...] = jnp.sum(energy_b[...], axis=0)
    pltpu.make_async_copy(others, others, en_sem.at[2]).wait()


def step_kernel(limit, momentum, update, energy, out, out_buf, sems):
    total = jnp.sum(energy[...], keepdims=True)
    shrink = jnp.minimum(1.0, limit / jnp.sqrt(total))
    steps = sems.shape[0]
    wide = momentum.shape[2] // steps
    copies = []
    for i in range(steps):
        span = pl.ds(i * wide, wide)
        rows = update[:, span].astype(jnp.float32)
        for q in range(OWNED):
            height = momentum.shape[1]
            out_buf[q, :, span] = 0.9 * momentum[q, :, span] + shrink * rows[q * height:(q + 1) * height]
        copies.append(pltpu.make_async_copy(out_buf.at[:, :, span], out.at[:, :, span], sems.at[i]))
        copies[-1].start()
    for copy in copies:
        copy.wait()


def body(gradients, keep_rows, keep_counts, momentum):
    _, all_rows, width = gradients.shape
    cols = width // TILE
    assert sum(CHUNKS) == cols
    cols_pad = -(-cols // 32) * 32
    cosine = cosine_table().astype(np.float32)
    tables = jnp.asarray(np.stack([cosine, cosine.T])).astype(jnp.bfloat16)
    full = SHARDS * width
    vmem = pl.BlockSpec(memory_space=pltpu.VMEM)
    anywhere = pl.BlockSpec(memory_space=pl.ANY)
    block = (REPS, cols, OWNED * KMAX, TILE)
    part = OWNED * TILE // SHARDS
    update, energy = pl.pallas_call(
        functools.partial(exchange_kernel, cols),
        out_shape=(
            jax.ShapeDtypeStruct((part, full), jnp.bfloat16),
            jax.ShapeDtypeStruct((1, TILE), jnp.float32),
        ),
        in_specs=[pl.BlockSpec(memory_space=pltpu.HBM)] * 4,
        out_specs=(anywhere, vmem),
        scratch_shapes=[
            pltpu.VMEM((all_rows, width), jnp.bfloat16),
            pltpu.VMEM(block, jnp.bfloat16),
            pltpu.VMEM(block, jnp.bfloat16),
            pltpu.VMEM((SHARDS, part, width), jnp.bfloat16),
            pltpu.VMEM((cols, ROW_TILES, KMAX), jnp.int32),
            pltpu.VMEM((ROW_TILES, cols), jnp.int32),
            pltpu.VMEM((2, TILE, TILE), jnp.bfloat16),
            pltpu.VMEM((cols * ROW_TILES, TILE), jnp.int32),
            pltpu.VMEM((4, cols_pad, TILE), jnp.int32),
            pltpu.VMEM((REPS, cols_pad // 2, TILE), jnp.bfloat16),
            pltpu.VMEM((REPS, cols_pad // 2, TILE), jnp.bfloat16),
            pltpu.VMEM((OWNED, 2, cols_pad, TILE), jnp.int32),
            pltpu.VMEM((8, TILE), jnp.float32),
            pltpu.VMEM((2, 1, TILE), jnp.float32),
            pltpu.VMEM((SHARDS, 1, TILE), jnp.float32),
            pltpu.VMEM((REPS, 1, TILE), jnp.float32),
            pltpu.SemaphoreType.DMA((len(CHUNKS),)),
            pltpu.SemaphoreType.DMA((3,)),
            pltpu.SemaphoreType.DMA((len(CHUNKS),)),
            pltpu.SemaphoreType.DMA((1,)),
            pltpu.SemaphoreType.DMA((2,)),
            pltpu.SemaphoreType.DMA((2,)),
            pltpu.SemaphoreType.DMA((4,)),
            pltpu.SemaphoreType.REGULAR,
        ],
        compiler_params=pltpu.CompilerParams(
            collective_id=0, has_side_effects=True, vmem_limit_bytes=48 * 1024 * 1024),
    )(gradients[0], jnp.transpose(keep_rows[0], (1, 0, 2)), keep_counts[0], tables)

    limit = math.sqrt(all_rows * full)
    return pl.pallas_call(
        functools.partial(step_kernel, limit),
        out_shape=jax.ShapeDtypeStruct(momentum.shape, momentum.dtype),
        in_specs=[vmem, vmem, vmem],
        out_specs=anywhere,
        scratch_shapes=[pltpu.VMEM(momentum.shape, jnp.float32), pltpu.SemaphoreType.DMA((8,))],
        compiler_params=pltpu.CompilerParams(vmem_limit_bytes=16 * 1024 * 1024),
    )(momentum, update, energy)


def solution(mesh):
    return jax.shard_map(
        body,
        mesh=mesh,
        in_specs=(
            P("rep", None, "shard"),
            P("rep", None, "shard", None),
            P("rep", None, "shard"),
            P("rep", "shard", None),
        ),
        out_specs=P("rep", "shard", None),
        check_vma=False,
    )
```

```python
import functools
import math

import jax
import jax.numpy as jnp
import numpy as np
from jax import lax
from jax.experimental import pallas as pl
from jax.experimental.pallas import tpu as pltpu
from jax.sharding import PartitionSpec as P

TILE = 128
KMAX = 32
REPS = 8
SHARDS = 16
ROW_TILES = 16
OWNED = ROW_TILES // REPS
CHUNKS = (1, 2, 4, 4, 4, 4, 4, 2, 2, 1, 1)
AHEAD = 3
PAIR = 2
MESH = pl.DeviceIdType.MESH


def cosine_table():
    freq = np.arange(TILE, dtype=np.float64)[:, None]
    place = np.arange(TILE, dtype=np.float64)[None, :]
    norming = np.where(freq == 0, math.sqrt(1.0 / TILE), math.sqrt(2.0 / TILE))
    return norming * np.cos(math.pi * (2.0 * place + 1.0) * freq / (2.0 * TILE))


def dot(a, b, dims=((1,), (0,))):
    return lax.dot_general(a, b, (dims, ((), ())), preferred_element_type=jnp.float32)


def exchange_kernel(
    cols, grads, keep_rows, keep_counts, tables, momentum, update, energy_out, momentum_near,
    x_buf, send_buf, recv_buf, upd_buf, rows_buf, counts_buf, tables_buf,
    lab_wide, lab_mine, lab_send, lab_recv, lab_own, energy, energy_row, energy_a, energy_b,
    x_sem, in_sem, blk_recv, blk_send, lab_sem, upd_sem, en_sem, near_sem, ready,
):
    shard = lax.axis_index("shard")
    rep = lax.axis_index("rep")
    starts = [sum(CHUNKS[:k]) for k in range(len(CHUNKS))]
    rep_peers = [lax.rem(rep // 2 + y, 4) * 2 + lax.rem(rep + core, 2)
                 for y in (2, 1, 3, 0) for core in (0, 1) if y or core]
    hops = sorted(((z, x) for z in range(4) for x in range(4) if z or x), key=lambda p: -(2 - abs(p[0] - 2)) - (2 - abs(p[1] - 2)))
    ring = [lax.rem(shard // 4 + z, 4) * 4 + lax.rem(shard + x, 4) for z, x in hops]
    shard_peers = [j + (j >= shard).astype(jnp.int32) for j in range(SHARDS - 1)]
    near = [peer for peer, (z, x) in zip(ring, hops) if not (z and x)]
    along_z = [peer for peer, (z, x) in zip(ring, hops) if not x]

    def x_copy(k):
        span = pl.ds(starts[k] * TILE, CHUNKS[k] * TILE)
        return pltpu.make_async_copy(grads.at[:, span], x_buf.at[:, span], x_sem.at[k])

    small = [
        pltpu.make_async_copy(keep_rows, rows_buf, in_sem.at[0]),
        pltpu.make_async_copy(keep_counts, counts_buf, in_sem.at[1]),
        pltpu.make_async_copy(tables, tables_buf, in_sem.at[2]),
    ]
    near_copy = pltpu.make_async_copy(momentum, momentum_near, near_sem.at[0])
    barrier = pltpu.get_barrier_semaphore()
    for peer in rep_peers:
        pl.semaphore_signal(barrier, inc=1, device_id=(shard, peer), device_id_type=MESH)
    for peer in near:
        pl.semaphore_signal(barrier, inc=1, device_id=(peer, rep), device_id_type=MESH)
    for copy in small:
        copy.start()
    x_copy(0).start()

    energy[...] = jnp.zeros_like(energy)
    for copy in small:
        copy.wait()
    table = tables_buf.at[0]
    table_t = tables_buf.at[1]

    def own_rows(first, count):
        for c in range(first, first + count):
            live = lax.broadcasted_iota(jnp.int32, (ROW_TILES, KMAX), 1) < counts_buf[:, c:c + 1]
            wide = jnp.where(live, rows_buf[c] + 1, 0)
            lab_wide[c * ROW_TILES:(c + 1) * ROW_TILES] = jnp.concatenate([wide] * 4, axis=1)
        slot = lax.broadcasted_iota(jnp.int32, (count, TILE), 1) // KMAX
        for group in range(4):
            row = jnp.zeros((count, TILE), jnp.int32)
            for t in range(4):
                got = lab_wide[pl.ds(first * ROW_TILES + 4 * group + t, count, stride=ROW_TILES), :]
                row = jnp.where(slot == t, got, row)
            lab_mine[group, first:first + count] = row

    def pack_rows():
        half = lab_send.shape[1]
        lower = lax.broadcasted_iota(jnp.int32, (half, TILE), 1) < TILE // 2
        for group in range(4):
            early, late = lab_mine[group, 0:half], lab_mine[group, half:2 * half]
            lab_send[2 * group] = jnp.where(lower, early, pltpu.roll(late, TILE // 2, 1)).astype(jnp.bfloat16)
            lab_send[2 * group + 1] = jnp.where(lower, pltpu.roll(early, TILE // 2, 1), late).astype(jnp.bfloat16)

    lab_mine[...] = jnp.zeros_like(lab_mine)
    own_rows(0, 1)
    x_copy(1).start()

    def lab_copy(peer):
        return pltpu.make_async_remote_copy(
            src_ref=lab_send.at[peer], dst_ref=lab_recv.at[rep],
            send_sem=lab_sem.at[0], recv_sem=lab_sem.at[1],
            device_id=(shard, peer), device_id_type=MESH)

    freq = lax.broadcasted_iota(jnp.int32, (TILE, TILE), 0) + 1

    def hits(row):
        return jnp.where(freq == row, 1.0, 0.0).astype(jnp.bfloat16)

    def encode(k):
        x_copy(k).wait()
        if k + 2 < len(CHUNKS):
            x_copy(k + 2).start()
        pair = min(PAIR, CHUNKS[k])

        def columns(step, carry):
            first = starts[k] + step * pair
            span = pl.ds(pl.multiple_of(first * TILE, TILE), pair * TILE)
            picks = [hits(lab_mine[group, pl.ds(first + i, 1), :]) for i in range(pair) for group in range(4)]
            left = dot(jnp.concatenate(picks, axis=1), table[...], ((0,), (0,))).astype(jnp.bfloat16)
            parts = [[None] * ROW_TILES for _ in range(pair)]
            for q in range(ROW_TILES):
                rows = [left[(i * ROW_TILES + q) * KMAX:(i * ROW_TILES + q + 1) * KMAX] for i in range(pair)]
                both = dot(jnp.concatenate(rows, axis=0), x_buf[q * TILE:(q + 1) * TILE, span])
                for i in range(pair):
                    parts[i][q] = both[i * KMAX:(i + 1) * KMAX, i * TILE:(i + 1) * TILE].astype(jnp.bfloat16)
            half = jnp.concatenate(parts[0] + (parts[1] if pair > 1 else []), axis=0)
            kept = dot(half, table_t[...]).astype(jnp.bfloat16)
            for i in range(pair):
                for peer in range(REPS):
                    at = (i * REPS + peer) * OWNED * KMAX
                    send_buf[peer, first + i] = kept[at:at + OWNED * KMAX]
            return carry

        lax.fori_loop(0, CHUNKS[k] // pair, columns, 0)

    def send_blocks(k):
        span = pl.ds(starts[k], CHUNKS[k])
        for peer in rep_peers:
            pltpu.make_async_remote_copy(
                src_ref=send_buf.at[peer, span], dst_ref=recv_buf.at[rep, span],
                send_sem=blk_send.at[0], recv_sem=blk_recv.at[k],
                device_id=(shard, peer), device_id_type=MESH).start()
        pltpu.make_async_copy(send_buf.at[rep, span], recv_buf.at[rep, span], blk_recv.at[k]).start()

    def own_labels():
        pltpu.make_async_copy(lab_recv, lab_recv, lab_sem.at[1]).wait()
        half = lab_send.shape[1]
        slot = lax.broadcasted_iota(jnp.int32, (half, TILE), 1) // KMAX
        for part in range(2):
            for group in range(2):
                for q in range(OWNED):
                    total = jnp.zeros((half, TILE), jnp.float32)
                    for i in range(4):
                        got = lab_recv[4 * group + i].astype(jnp.float32)
                        shift = (i - q - 2 * part) % 4 * KMAX
                        moved = pltpu.roll(got, shift, 1) if shift else got
                        total = jnp.where(slot == i, moved, total)
                    lab_own[q, group, part * half:(part + 1) * half] = total.astype(jnp.int32)

    def decode(k, summed_up=None):
        span = pl.ds(starts[k], CHUNKS[k])
        pltpu.make_async_copy(recv_buf.at[:, span], recv_buf.at[:, span], blk_recv.at[k]).wait()

        pair = min(PAIR, CHUNKS[k])

        def columns(step, carry):
            first = starts[k] + step * pair
            sums = []
            for i in range(pair):
                for q in range(OWNED):
                    places = jnp.concatenate(
                        [hits(lab_own[q, half, pl.ds(first + i, 1), :]) for half in range(2)], axis=1)
                    block = recv_buf[:, first + i, q * KMAX:(q + 1) * KMAX, :].reshape(REPS * KMAX, TILE)
                    sums.append(dot(places, block))
            squares = sum(jnp.sum((v * v).reshape(TILE // 8, 8, TILE), axis=0) for v in sums)
            energy[...] += squares
            if summed_up is not None:
                summed_up()
            wide = jnp.concatenate([v.astype(jnp.bfloat16) for v in sums], axis=1)
            rows = dot(table_t[...], wide).astype(jnp.bfloat16)
            tall = jnp.concatenate([rows[:, n * TILE:(n + 1) * TILE] for n in range(len(sums))], axis=0)
            done = dot(tall, table[...]).reshape(len(sums), SHARDS, TILE // SHARDS, TILE)
            for i in range(pair):
                both = jnp.concatenate([done[i * OWNED + q] for q in range(OWNED)], axis=1).astype(jnp.bfloat16)
                upd_buf[:, :, pl.ds(pl.multiple_of((first + i) * TILE, TILE), TILE)] = both
            return carry

        if CHUNKS[k] == pair:
            columns(0, 0)
        else:
            lax.fori_loop(0, CHUNKS[k] // pair, columns, 0)

    def send_update(k):
        width = CHUNKS[k] * TILE
        src = pl.ds(starts[k] * TILE, width)
        dst = pl.ds(pl.multiple_of((shard * cols + starts[k]) * TILE, TILE), width)
        for peer in shard_peers:
            pltpu.make_async_remote_copy(
                src_ref=upd_buf.at[peer, :, src], dst_ref=update.at[:, dst],
                send_sem=upd_sem.at[0], recv_sem=upd_sem.at[1],
                device_id=(peer, rep), device_id_type=MESH).start()
        pltpu.make_async_copy(upd_buf.at[shard, :, src], update.at[:, dst], upd_sem.at[1]).start()

    def send_energy():
        energy_row[0] = jnp.sum(energy[...], axis=0, keepdims=True)
        energy_b[rep] = energy_row[0]
        for peer in rep_peers:
            pltpu.make_async_remote_copy(
                src_ref=energy_row.at[0], dst_ref=energy_b.at[rep],
                send_sem=en_sem.at[2], recv_sem=en_sem.at[3],
                device_id=(shard, peer), device_id_type=MESH).start()

    last = len(CHUNKS)
    encode(0)
    pl.semaphore_wait(barrier, REPS - 1 + len(near))
    send_blocks(0)
    own_rows(1, cols - 1)
    encode(1)
    send_blocks(1)
    pack_rows()
    for peer in rep_peers:
        lab_copy(peer).start()
    pltpu.make_async_copy(lab_send.at[rep], lab_recv.at[rep], lab_sem.at[1]).start()
    for peer in along_z:
        pl.semaphore_signal(ready, inc=1, device_id=(peer, rep), device_id_type=MESH)
    for k in range(2, AHEAD):
        encode(k)
        send_blocks(k)
    for k in range(last):
        if k + AHEAD < last:
            encode(k + AHEAD)
            send_blocks(k + AHEAD)
        if k == 0:
            own_labels()
        if k == 1:
            near_copy.start()
        decode(k, send_energy if k == last - 1 else None)
        if k == 0:
            pl.semaphore_wait(ready, len(along_z))
        send_update(k)

    sent = send_buf.at[pl.ds(0, REPS - 1)]
    pltpu.make_async_copy(sent, sent, blk_send.at[0]).wait()
    near_copy.wait()
    over_rep = energy_b.at[pl.ds(0, REPS - 1)]
    pltpu.make_async_copy(over_rep, over_rep, en_sem.at[3]).wait()
    energy_row[1] = jnp.sum(energy_b[...], axis=0)
    energy_a[shard] = energy_row[1]
    for peer in shard_peers:
        pltpu.make_async_remote_copy(
            src_ref=energy_row.at[1], dst_ref=energy_a.at[shard],
            send_sem=en_sem.at[0], recv_sem=en_sem.at[1],
            device_id=(peer, rep), device_id_type=MESH).start()
    sent = lab_recv.at[pl.ds(0, REPS - 1)]
    pltpu.make_async_copy(sent, sent, lab_sem.at[0]).wait()
    pltpu.make_async_copy(over_rep, over_rep, en_sem.at[2]).wait()
    sent = upd_buf.at[pl.ds(0, SHARDS - 1)]
    pltpu.make_async_copy(sent, sent, upd_sem.at[0]).wait()
    pltpu.make_async_copy(upd_buf, upd_buf, upd_sem.at[1]).wait()
    over_shard = energy_a.at[pl.ds(0, SHARDS - 1)]
    pltpu.make_async_copy(over_shard, over_shard, en_sem.at[1]).wait()
    energy_out[...] = jnp.sum(energy_a[...], axis=0)
    pltpu.make_async_copy(over_shard, over_shard, en_sem.at[0]).wait()


def step_kernel(limit, momentum, update, energy, out, out_buf, sems):
    total = jnp.sum(energy[...], keepdims=True)
    shrink = jnp.minimum(1.0, limit / jnp.sqrt(total))
    steps = sems.shape[0]
    wide = momentum.shape[2] // steps
    copies = []
    for i in range(steps):
        span = pl.ds(i * wide, wide)
        rows = update[:, span].astype(jnp.float32)
        for q in range(OWNED):
            height = momentum.shape[1]
            out_buf[q, :, span] = 0.9 * momentum[q, :, span] + shrink * rows[q * height:(q + 1) * height]
        copies.append(pltpu.make_async_copy(out_buf.at[:, :, span], out.at[:, :, span], sems.at[i]))
        copies[-1].start()
    for copy in copies:
        copy.wait()


def body(gradients, keep_rows, keep_counts, momentum):
    _, all_rows, width = gradients.shape
    cols = width // TILE
    assert sum(CHUNKS) == cols
    cols_pad = -(-cols // 32) * 32
    cosine = cosine_table().astype(np.float32)
    tables = jnp.asarray(np.stack([cosine, cosine.T])).astype(jnp.bfloat16)
    full = SHARDS * width
    vmem = pl.BlockSpec(memory_space=pltpu.VMEM)
    anywhere = pl.BlockSpec(memory_space=pl.ANY)
    block = (REPS, cols, OWNED * KMAX, TILE)
    part = OWNED * TILE // SHARDS
    update, energy, momentum_near = pl.pallas_call(
        functools.partial(exchange_kernel, cols),
        out_shape=(
            jax.ShapeDtypeStruct((part, full), jnp.bfloat16),
            jax.ShapeDtypeStruct((1, TILE), jnp.float32),
            jax.ShapeDtypeStruct(momentum.shape, jnp.float32),
        ),
        in_specs=[pl.BlockSpec(memory_space=pltpu.HBM)] * 5,
        out_specs=(anywhere, vmem, anywhere),
        scratch_shapes=[
            pltpu.VMEM((all_rows, width), jnp.bfloat16),
            pltpu.VMEM(block, jnp.bfloat16),
            pltpu.VMEM(block, jnp.bfloat16),
            pltpu.VMEM((SHARDS, part, width), jnp.bfloat16),
            pltpu.VMEM((cols, ROW_TILES, KMAX), jnp.int32),
            pltpu.VMEM((ROW_TILES, cols), jnp.int32),
            pltpu.VMEM((2, TILE, TILE), jnp.bfloat16),
            pltpu.VMEM(((cols + 1) * ROW_TILES, TILE), jnp.int32),
            pltpu.VMEM((4, cols_pad, TILE), jnp.int32),
            pltpu.VMEM((REPS, cols_pad // 2, TILE), jnp.bfloat16),
            pltpu.VMEM((REPS, cols_pad // 2, TILE), jnp.bfloat16),
            pltpu.VMEM((OWNED, 2, cols_pad, TILE), jnp.int32),
            pltpu.VMEM((8, TILE), jnp.float32),
            pltpu.VMEM((2, 1, TILE), jnp.float32),
            pltpu.VMEM((SHARDS, 1, TILE), jnp.float32),
            pltpu.VMEM((REPS, 1, TILE), jnp.float32),
            pltpu.SemaphoreType.DMA((len(CHUNKS),)),
            pltpu.SemaphoreType.DMA((3,)),
            pltpu.SemaphoreType.DMA((len(CHUNKS),)),
            pltpu.SemaphoreType.DMA((1,)),
            pltpu.SemaphoreType.DMA((2,)),
            pltpu.SemaphoreType.DMA((2,)),
            pltpu.SemaphoreType.DMA((4,)),
            pltpu.SemaphoreType.DMA((1,)),
            pltpu.SemaphoreType.REGULAR,
        ],
        compiler_params=pltpu.CompilerParams(
            collective_id=0, has_side_effects=True, vmem_limit_bytes=48 * 1024 * 1024),
    )(*[pltpu.with_memory_space_constraint(v, pltpu.HBM) for v in (
        gradients[0], jnp.transpose(keep_rows[0], (1, 0, 2)), keep_counts[0], tables, momentum)])

    limit = math.sqrt(all_rows * full)
    return pl.pallas_call(
        functools.partial(step_kernel, limit),
        out_shape=jax.ShapeDtypeStruct(momentum.shape, momentum.dtype),
        in_specs=[vmem, vmem, vmem],
        out_specs=anywhere,
        scratch_shapes=[pltpu.VMEM(momentum.shape, jnp.float32), pltpu.SemaphoreType.DMA((8,))],
        compiler_params=pltpu.CompilerParams(vmem_limit_bytes=16 * 1024 * 1024),
    )(momentum_near, update, energy)


def solution(mesh):
    return jax.shard_map(
        body,
        mesh=mesh,
        in_specs=(
            P("rep", None, "shard"),
            P("rep", None, "shard", None),
            P("rep", None, "shard"),
            P("rep", "shard", None),
        ),
        out_specs=P("rep", "shard", None),
        check_vma=False,
    )
```

```python
import functools
import math

import jax
import jax.numpy as jnp
import numpy as np
from jax import lax
from jax.experimental import pallas as pl
from jax.experimental.pallas import tpu as pltpu
from jax.sharding import PartitionSpec as P

TILE = 128
KMAX = 32
REPS = 8
SHARDS = 16
ROW_TILES = 16
OWNED = ROW_TILES // REPS
CHUNKS = (1, 2, 4, 4, 4, 4, 4, 2, 2, 1, 1)
AHEAD = 3
PAIR = 2
MESH = pl.DeviceIdType.MESH


def cosine_table():
    freq = np.arange(TILE, dtype=np.float64)[:, None]
    place = np.arange(TILE, dtype=np.float64)[None, :]
    norming = np.where(freq == 0, math.sqrt(1.0 / TILE), math.sqrt(2.0 / TILE))
    return norming * np.cos(math.pi * (2.0 * place + 1.0) * freq / (2.0 * TILE))


def dot(a, b, dims=((1,), (0,))):
    return lax.dot_general(a, b, (dims, ((), ())), preferred_element_type=jnp.float32)


def exchange_kernel(
    cols, grads, keep_rows, keep_counts, tables, momentum, update, energy_out, momentum_near,
    x_buf, send_buf, recv_buf, upd_buf, rows_buf, counts_buf, tables_buf,
    lab_wide, lab_mine, lab_send, lab_recv, lab_own, energy, energy_row, energy_a, energy_b,
    x_sem, in_sem, blk_recv, blk_send, lab_sem, upd_sem, en_sem, near_sem, ready,
):
    shard = lax.axis_index("shard")
    rep = lax.axis_index("rep")
    starts = [sum(CHUNKS[:k]) for k in range(len(CHUNKS))]
    rep_peers = [lax.rem(rep // 2 + y, 4) * 2 + lax.rem(rep + core, 2)
                 for y in (2, 1, 3, 0) for core in (0, 1) if y or core]
    hops = sorted(((z, x) for z in range(4) for x in range(4) if z or x), key=lambda p: -(2 - abs(p[0] - 2)) - (2 - abs(p[1] - 2)))
    ring = [lax.rem(shard // 4 + z, 4) * 4 + lax.rem(shard + x, 4) for z, x in hops]
    shard_peers = ring
    near = [peer for peer, (z, x) in zip(ring, hops) if not (z and x)]
    along_z = [peer for peer, (z, x) in zip(ring, hops) if not x]

    def x_copy(k):
        span = pl.ds(starts[k] * TILE, CHUNKS[k] * TILE)
        return pltpu.make_async_copy(grads.at[:, span], x_buf.at[:, span], x_sem.at[k])

    small = [
        pltpu.make_async_copy(keep_rows, rows_buf, in_sem.at[0]),
        pltpu.make_async_copy(keep_counts, counts_buf, in_sem.at[1]),
        pltpu.make_async_copy(tables, tables_buf, in_sem.at[2]),
    ]
    near_copy = pltpu.make_async_copy(momentum, momentum_near, near_sem.at[0])
    barrier = pltpu.get_barrier_semaphore()
    for peer in rep_peers:
        pl.semaphore_signal(barrier, inc=1, device_id=(shard, peer), device_id_type=MESH)
    for peer in near:
        pl.semaphore_signal(barrier, inc=1, device_id=(peer, rep), device_id_type=MESH)
    for copy in small:
        copy.start()
    x_copy(0).start()

    energy[...] = jnp.zeros_like(energy)
    for copy in small:
        copy.wait()
    table = tables_buf.at[0]
    table_t = tables_buf.at[1]

    def own_rows(first, count):
        for c in range(first, first + count):
            live = lax.broadcasted_iota(jnp.int32, (ROW_TILES, KMAX), 1) < counts_buf[:, c:c + 1]
            wide = jnp.where(live, rows_buf[c] + 1, 0)
            lab_wide[c * ROW_TILES:(c + 1) * ROW_TILES] = jnp.concatenate([wide] * 4, axis=1)
        slot = lax.broadcasted_iota(jnp.int32, (count, TILE), 1) // KMAX
        for group in range(4):
            row = jnp.zeros((count, TILE), jnp.int32)
            for t in range(4):
                got = lab_wide[pl.ds(first * ROW_TILES + 4 * group + t, count, stride=ROW_TILES), :]
                row = jnp.where(slot == t, got, row)
            lab_mine[group, first:first + count] = row

    def pack_rows():
        half = lab_send.shape[1]
        lower = lax.broadcasted_iota(jnp.int32, (half, TILE), 1) < TILE // 2
        for group in range(4):
            early, late = lab_mine[group, 0:half], lab_mine[group, half:2 * half]
            lab_send[2 * group] = jnp.where(lower, early, pltpu.roll(late, TILE // 2, 1)).astype(jnp.bfloat16)
            lab_send[2 * group + 1] = jnp.where(lower, pltpu.roll(early, TILE // 2, 1), late).astype(jnp.bfloat16)

    lab_mine[...] = jnp.zeros_like(lab_mine)
    own_rows(0, 1)
    x_copy(1).start()

    def lab_copy(peer):
        return pltpu.make_async_remote_copy(
            src_ref=lab_send.at[peer], dst_ref=lab_recv.at[rep],
            send_sem=lab_sem.at[0], recv_sem=lab_sem.at[1],
            device_id=(shard, peer), device_id_type=MESH)

    freq = lax.broadcasted_iota(jnp.int32, (TILE, TILE), 0) + 1

    def hits(row):
        return jnp.where(freq == row, 1.0, 0.0).astype(jnp.bfloat16)

    def encode(k):
        x_copy(k).wait()
        if k + 2 < len(CHUNKS):
            x_copy(k + 2).start()
        pair = min(PAIR, CHUNKS[k])

        def columns(step, carry):
            first = starts[k] + step * pair
            span = pl.ds(pl.multiple_of(first * TILE, TILE), pair * TILE)
            picks = [hits(lab_mine[group, pl.ds(first + i, 1), :]) for i in range(pair) for group in range(4)]
            left = dot(jnp.concatenate(picks, axis=1), table[...], ((0,), (0,))).astype(jnp.bfloat16)
            parts = [[None] * ROW_TILES for _ in range(pair)]
            for q in range(ROW_TILES):
                rows = [left[(i * ROW_TILES + q) * KMAX:(i * ROW_TILES + q + 1) * KMAX] for i in range(pair)]
                both = dot(jnp.concatenate(rows, axis=0), x_buf[q * TILE:(q + 1) * TILE, span])
                for i in range(pair):
                    parts[i][q] = both[i * KMAX:(i + 1) * KMAX, i * TILE:(i + 1) * TILE].astype(jnp.bfloat16)
            half = jnp.concatenate(parts[0] + (parts[1] if pair > 1 else []), axis=0)
            kept = dot(half, table_t[...]).astype(jnp.bfloat16)
            for i in range(pair):
                for peer in range(REPS):
                    at = (i * REPS + peer) * OWNED * KMAX
                    send_buf[peer, first + i] = kept[at:at + OWNED * KMAX]
            return carry

        lax.fori_loop(0, CHUNKS[k] // pair, columns, 0)

    def send_blocks(k):
        span = pl.ds(starts[k], CHUNKS[k])
        for peer in rep_peers:
            pltpu.make_async_remote_copy(
                src_ref=send_buf.at[peer, span], dst_ref=recv_buf.at[rep, span],
                send_sem=blk_send.at[0], recv_sem=blk_recv.at[k],
                device_id=(shard, peer), device_id_type=MESH).start()
        pltpu.make_async_copy(send_buf.at[rep, span], recv_buf.at[rep, span], blk_recv.at[k]).start()

    def own_labels():
        pltpu.make_async_copy(lab_recv, lab_recv, lab_sem.at[1]).wait()
        half = lab_send.shape[1]
        slot = lax.broadcasted_iota(jnp.int32, (half, TILE), 1) // KMAX
        for part in range(2):
            for group in range(2):
                for q in range(OWNED):
                    total = jnp.zeros((half, TILE), jnp.float32)
                    for i in range(4):
                        got = lab_recv[4 * group + i].astype(jnp.float32)
                        shift = (i - q - 2 * part) % 4 * KMAX
                        moved = pltpu.roll(got, shift, 1) if shift else got
                        total = jnp.where(slot == i, moved, total)
                    lab_own[q, group, part * half:(part + 1) * half] = total.astype(jnp.int32)

    def places(column, q):
        return jnp.concatenate([hits(lab_own[q, half, pl.ds(column, 1), :]) for half in range(2)], axis=1)

    def decode(k, summed_up=None):
        span = pl.ds(starts[k], CHUNKS[k])
        pair = min(PAIR, CHUNKS[k])
        ready_places = [places(starts[k] + i, q) for i in range(pair) for q in range(OWNED)] if CHUNKS[k] == pair else None
        pltpu.make_async_copy(recv_buf.at[:, span], recv_buf.at[:, span], blk_recv.at[k]).wait()

        def columns(step, carry):
            first = starts[k] + step * pair
            sums = []
            for i in range(pair):
                for q in range(OWNED):
                    where = ready_places[i * OWNED + q] if ready_places else places(first + i, q)
                    block = recv_buf[:, first + i, q * KMAX:(q + 1) * KMAX, :].reshape(REPS * KMAX, TILE)
                    sums.append(dot(where, block))
            squares = sum(jnp.sum((v * v).reshape(TILE // 8, 8, TILE), axis=0) for v in sums)
            energy[...] += squares
            if summed_up is not None:
                summed_up()
            wide = jnp.concatenate([v.astype(jnp.bfloat16) for v in sums], axis=1)
            rows = dot(table_t[...], wide).astype(jnp.bfloat16)
            tall = jnp.concatenate([rows[:, n * TILE:(n + 1) * TILE] for n in range(len(sums))], axis=0)
            done = dot(tall, table[...]).reshape(len(sums), SHARDS, TILE // SHARDS, TILE)
            for i in range(pair):
                both = jnp.concatenate([done[i * OWNED + q] for q in range(OWNED)], axis=1).astype(jnp.bfloat16)
                upd_buf[:, :, pl.ds(pl.multiple_of((first + i) * TILE, TILE), TILE)] = both
            return carry

        if CHUNKS[k] == pair:
            columns(0, 0)
        else:
            lax.fori_loop(0, CHUNKS[k] // pair, columns, 0)

    def send_update(k):
        width = CHUNKS[k] * TILE
        src = pl.ds(starts[k] * TILE, width)
        dst = pl.ds(pl.multiple_of((shard * cols + starts[k]) * TILE, TILE), width)
        for peer in shard_peers:
            pltpu.make_async_remote_copy(
                src_ref=upd_buf.at[peer, :, src], dst_ref=update.at[:, dst],
                send_sem=upd_sem.at[0], recv_sem=upd_sem.at[1],
                device_id=(peer, rep), device_id_type=MESH).start()
        pltpu.make_async_copy(upd_buf.at[shard, :, src], update.at[:, dst], upd_sem.at[1]).start()

    def send_energy():
        energy_row[0] = jnp.sum(energy[...], axis=0, keepdims=True)
        energy_b[rep] = energy_row[0]
        for peer in rep_peers:
            pltpu.make_async_remote_copy(
                src_ref=energy_row.at[0], dst_ref=energy_b.at[rep],
                send_sem=en_sem.at[2], recv_sem=en_sem.at[3],
                device_id=(shard, peer), device_id_type=MESH).start()

    last = len(CHUNKS)
    encode(0)
    pl.semaphore_wait(barrier, REPS - 1 + len(near))
    send_blocks(0)
    own_rows(1, cols - 1)
    encode(1)
    send_blocks(1)
    pack_rows()
    for peer in rep_peers:
        lab_copy(peer).start()
    pltpu.make_async_copy(lab_send.at[rep], lab_recv.at[rep], lab_sem.at[1]).start()
    for peer in along_z:
        pl.semaphore_signal(ready, inc=1, device_id=(peer, rep), device_id_type=MESH)
    for k in range(2, AHEAD):
        encode(k)
        send_blocks(k)
    for k in range(last):
        if k + AHEAD < last:
            encode(k + AHEAD)
            send_blocks(k + AHEAD)
        if k == 0:
            own_labels()
        if k == 1:
            near_copy.start()
        decode(k, send_energy if k == last - 1 else None)
        if k == 0:
            pl.semaphore_wait(ready, len(along_z))
        send_update(k)

    sent = send_buf.at[pl.ds(0, REPS - 1)]
    pltpu.make_async_copy(sent, sent, blk_send.at[0]).wait()
    near_copy.wait()
    over_rep = energy_b.at[pl.ds(0, REPS - 1)]
    pltpu.make_async_copy(over_rep, over_rep, en_sem.at[3]).wait()
    energy_row[1] = jnp.sum(energy_b[...], axis=0)
    energy_a[shard] = energy_row[1]
    for peer in shard_peers:
        pltpu.make_async_remote_copy(
            src_ref=energy_row.at[1], dst_ref=energy_a.at[shard],
            send_sem=en_sem.at[0], recv_sem=en_sem.at[1],
            device_id=(peer, rep), device_id_type=MESH).start()
    sent = lab_recv.at[pl.ds(0, REPS - 1)]
    pltpu.make_async_copy(sent, sent, lab_sem.at[0]).wait()
    pltpu.make_async_copy(over_rep, over_rep, en_sem.at[2]).wait()
    sent = upd_buf.at[pl.ds(0, SHARDS - 1)]
    pltpu.make_async_copy(sent, sent, upd_sem.at[0]).wait()
    pltpu.make_async_copy(upd_buf, upd_buf, upd_sem.at[1]).wait()
    over_shard = energy_a.at[pl.ds(0, SHARDS - 1)]
    pltpu.make_async_copy(over_shard, over_shard, en_sem.at[1]).wait()
    energy_out[...] = jnp.sum(energy_a[...], axis=0)
    pltpu.make_async_copy(over_shard, over_shard, en_sem.at[0]).wait()


def step_kernel(limit, momentum, update, energy, out, out_buf, sems):
    total = jnp.sum(energy[...], keepdims=True)
    shrink = jnp.minimum(1.0, limit / jnp.sqrt(total))
    steps = sems.shape[0]
    wide = momentum.shape[2] // steps
    copies = []
    for i in range(steps):
        span = pl.ds(i * wide, wide)
        rows = update[:, span].astype(jnp.float32)
        for q in range(OWNED):
            height = momentum.shape[1]
            out_buf[q, :, span] = 0.9 * momentum[q, :, span] + shrink * rows[q * height:(q + 1) * height]
        copies.append(pltpu.make_async_copy(out_buf.at[:, :, span], out.at[:, :, span], sems.at[i]))
        copies[-1].start()
    for copy in copies:
        copy.wait()


def body(gradients, keep_rows, keep_counts, momentum):
    _, all_rows, width = gradients.shape
    cols = width // TILE
    assert sum(CHUNKS) == cols
    cols_pad = -(-cols // 32) * 32
    cosine = cosine_table().astype(np.float32)
    tables = jnp.asarray(np.stack([cosine, cosine.T])).astype(jnp.bfloat16)
    full = SHARDS * width
    vmem = pl.BlockSpec(memory_space=pltpu.VMEM)
    anywhere = pl.BlockSpec(memory_space=pl.ANY)
    block = (REPS, cols, OWNED * KMAX, TILE)
    part = OWNED * TILE // SHARDS
    update, energy, momentum_near = pl.pallas_call(
        functools.partial(exchange_kernel, cols),
        out_shape=(
            jax.ShapeDtypeStruct((part, full), jnp.bfloat16),
            jax.ShapeDtypeStruct((1, TILE), jnp.float32),
            jax.ShapeDtypeStruct(momentum.shape, jnp.float32),
        ),
        in_specs=[pl.BlockSpec(memory_space=pltpu.HBM)] * 5,
        out_specs=(anywhere, vmem, anywhere),
        scratch_shapes=[
            pltpu.VMEM((all_rows, width), jnp.bfloat16),
            pltpu.VMEM(block, jnp.bfloat16),
            pltpu.VMEM(block, jnp.bfloat16),
            pltpu.VMEM((SHARDS, part, width), jnp.bfloat16),
            pltpu.VMEM((cols, ROW_TILES, KMAX), jnp.int32),
            pltpu.VMEM((ROW_TILES, cols), jnp.int32),
            pltpu.VMEM((2, TILE, TILE), jnp.bfloat16),
            pltpu.VMEM(((cols + 1) * ROW_TILES, TILE), jnp.int32),
            pltpu.VMEM((4, cols_pad, TILE), jnp.int32),
            pltpu.VMEM((REPS, cols_pad // 2, TILE), jnp.bfloat16),
            pltpu.VMEM((REPS, cols_pad // 2, TILE), jnp.bfloat16),
            pltpu.VMEM((OWNED, 2, cols_pad, TILE), jnp.int32),
            pltpu.VMEM((8, TILE), jnp.float32),
            pltpu.VMEM((2, 1, TILE), jnp.float32),
            pltpu.VMEM((SHARDS, 1, TILE), jnp.float32),
            pltpu.VMEM((REPS, 1, TILE), jnp.float32),
            pltpu.SemaphoreType.DMA((len(CHUNKS),)),
            pltpu.SemaphoreType.DMA((3,)),
            pltpu.SemaphoreType.DMA((len(CHUNKS),)),
            pltpu.SemaphoreType.DMA((1,)),
            pltpu.SemaphoreType.DMA((2,)),
            pltpu.SemaphoreType.DMA((2,)),
            pltpu.SemaphoreType.DMA((4,)),
            pltpu.SemaphoreType.DMA((1,)),
            pltpu.SemaphoreType.REGULAR,
        ],
        compiler_params=pltpu.CompilerParams(
            collective_id=0, has_side_effects=True, vmem_limit_bytes=48 * 1024 * 1024),
    )(*[pltpu.with_memory_space_constraint(v, pltpu.HBM) for v in (
        gradients[0], jnp.transpose(keep_rows[0], (1, 0, 2)), keep_counts[0], tables, momentum)])

    limit = math.sqrt(all_rows * full)
    return pl.pallas_call(
        functools.partial(step_kernel, limit),
        out_shape=jax.ShapeDtypeStruct(momentum.shape, momentum.dtype),
        in_specs=[vmem, vmem, vmem],
        out_specs=anywhere,
        scratch_shapes=[pltpu.VMEM(momentum.shape, jnp.float32), pltpu.SemaphoreType.DMA((8,))],
        compiler_params=pltpu.CompilerParams(vmem_limit_bytes=16 * 1024 * 1024),
    )(momentum_near, update, energy)


def solution(mesh):
    return jax.shard_map(
        body,
        mesh=mesh,
        in_specs=(
            P("rep", None, "shard"),
            P("rep", None, "shard", None),
            P("rep", None, "shard"),
            P("rep", "shard", None),
        ),
        out_specs=P("rep", "shard", None),
        check_vma=False,
    )
```
